32 devices in a mesh: ctx: 32 (over z, y, x, core), head: 1.
Axes of the slice: x: 2, y: 2, z: 4, core: 2. Of those that a mesh axis runs over, the one named last changes fastest.
Arguments:
- queries: bfloat16 [256, 4096], P('head', 'ctx'), may hold values from -6 to 6
- keys: bfloat16 [256, 4096], P('head', 'ctx'), may hold values from -6 to 6
- values: bfloat16 [4096, 2048], P('ctx', 'head'), may hold values from -6 to 6
- seg_ids: int32 [4096], P('ctx'), may hold values from 0 to 3, never falling along the last dimension, each value on 1 to 2048 neighbouring positions
- conv_weight: bfloat16 [3, 256], P(None, 'head'), may hold values from -3.5 to 3.5
- out_weight: bfloat16 [2048, 4096], P('head'), may hold values from -0.125 to 0.125
- out_grad: bfloat16 [4096, 4096], P('ctx', 'head'), may hold values from -6 to 6
Outputs:
- grad_queries: float32 [256, 4096], P('head', 'ctx')
- grad_keys: float32 [256, 4096], P('head', 'ctx')
- grad_values: float32 [4096, 2048], P('ctx', 'head')
The draws below stay inside these ranges and needn't reach their ends.
Inputs may be any that keep to these rules, and one draw needn't show every extreme that they name: `seg_ids`: document numbers never fall along the sequence; each document holds 1 to 2048 tokens, and one holds exactly 2048.
All inputs are finite; a program needn't handle non-finite values.
Results may differ from the reference program's by a relative error of at most 0.0005.
Values may be sent and summed in bfloat16 or wider, within the bound.
A program may use at most 128 MiB of HBM per device.

```python
import math
import jax
import jax.numpy as jnp
import numpy as np
from jax import lax

D = 4096
HEADS = 16
HD = 128
FD = 16
TOK_DEV = 128
NF = 153
QK = 256
HV = 2048
SEQ = 4096
MOST = 2048
DOCS = 4


def steps_of(stream_key, extent, pieces, smallest, largest):
    factor_of = 1.0
    for position, blocks in pieces:
        steps = jax.random.uniform(jax.random.fold_in(jax.random.fold_in(stream_key, 6), position), (blocks,), jnp.float32, smallest / len(pieces), largest / len(pieces))
        factor_of = factor_of * jnp.repeat(jnp.exp(steps), extent[position] // blocks).reshape((-1,) + (1,) * (len(extent) - 1 - position))
    return factor_of


def split_up(amount, total, reach, slope):
    portions = [(1 << 20) // math.isqrt(grade ** slope) + 1 for grade in range(2, amount + 1)]
    surplus, given = total - reach - (amount - 1), [1] * (amount - 1)
    while surplus > 0:
        candidates = [i for i in range(amount - 1) if given[i] < reach]
        pool, left = sum([portions[i] for i in candidates]), surplus
        for i in candidates:
            addition = min(reach - given[i], max(1, left * portions[i] // pool), surplus)
            given[i] = given[i] + addition
            surplus = surplus - addition
    return np.array([reach] + given)


def uneven(stream_key, count, total, limit, slope):
    if count == 2:
        one = jax.random.randint(stream_key, (), max(1, total - limit), min(limit, total - 1) + 1)
        return jnp.stack([one, total - one])
    tallies = jnp.asarray(split_up(count, total, limit, slope), jnp.int32)
    twos = (count - 1) // 2
    donor, taker = tallies[1:1 + 2 * twos:2], tallies[2:2 + 2 * twos:2]
    slack = jnp.minimum(donor - 1, limit - taker)
    moved = jax.random.randint(jax.random.fold_in(stream_key, 1), (twos,), 0, 1 << 20) % (slack + 1)
    tallies = tallies.at[1:1 + 2 * twos:2].set(donor - moved).at[2:2 + 2 * twos:2].set(taker + moved)
    return tallies[jax.random.permutation(jax.random.fold_in(stream_key, 2), count)]


def scatter_about(rng, dims, deviation, bound, split=(), kind=jnp.bfloat16):
    values = jax.random.normal(rng, dims, jnp.float32) * deviation
    if len(split) > 0:
        values = steps_of(rng, dims, split, -0.22, 0.18) * values
    return jnp.clip(values, min=-bound, max=bound).astype(kind)


def setup_inputs(seed: int = 0) -> dict:
    seeds = jax.random.split(jax.random.key(seed), 8)
    queries = scatter_about(seeds[0], (QK, SEQ), 1.0, 6.0, ((1, 32),))
    keys = scatter_about(seeds[1], (QK, SEQ), 1.0, 6.0, ((1, 32),))
    values = scatter_about(seeds[2], (SEQ, HV), 1.0, 6.0, ((0, 32),))
    seg_ids = jnp.searchsorted(jnp.cumsum(uneven(seeds[3], DOCS, SEQ, MOST, 2)), jnp.arange(SEQ), side="right").astype(jnp.int32)
    conv_weight = scatter_about(seeds[4], (3, QK), 3 ** -0.5, 3.5)
    out_weight = scatter_about(seeds[5], (HV, D), HV ** -0.5, 0.125)
    out_grad = scatter_about(seeds[6], (SEQ, D), 1.0, 6.0, ((0, 32),))
    return dict(queries=queries, keys=keys, values=values, seg_ids=seg_ids, conv_weight=conv_weight, out_weight=out_weight, out_grad=out_grad)


half_root = 0.7071067811865476
exact_mode = lax.Precision.HIGHEST

def features(entries):
    scaled = entries * 0.5
    row_index, col_index = np.triu_indices(scaled.shape[-2], 1)
    cross = jnp.take(scaled, row_index, axis=-2) * jnp.take(scaled, col_index, axis=-2)
    return jnp.concatenate([jnp.ones_like(scaled[..., :1, :]), scaled, scaled * scaled * half_root, cross], axis=-2)

def block_output(q_feat, k_feat, head_values, doc_ids, carry_mask, state_in, normer_in):
    length = doc_ids.shape[0]
    causal = jnp.arange(length)[:, None] >= jnp.arange(length)[None, :]
    allowed = (causal & (doc_ids[:, None] == doc_ids[None, :])).astype(jnp.float32)
    scores = jnp.einsum('hft,hfs->hts', q_feat, k_feat, precision=exact_mode) * allowed[None, :, :]
    numerator = jnp.einsum('hts,shd->thd', scores, head_values, precision=exact_mode)
    numerator = numerator + carry_mask[:, None, None] * jnp.einsum('hft,hfd->thd', q_feat, state_in, precision=exact_mode)
    denominator = lax.optimization_barrier(jnp.sum(scores, axis=2)).T + carry_mask[:, None] * jnp.einsum('hft,hf->th', q_feat, normer_in, precision=exact_mode)
    return numerator / denominator[:, :, None]

def convolve(query_rows, taps, doc_ids):
    summed = taps[0][:, None] * query_rows
    for offset in (1, 2):
        shifted = jnp.pad(query_rows, ((0, 0), (offset, 0)))[:, :-offset]
        shifted_ids = jnp.pad(doc_ids, (offset, 0), constant_values=-1)[:-offset]
        same_doc = (shifted_ids == doc_ids).astype(jnp.float32)
        summed = summed + taps[offset][:, None] * shifted * same_doc[None, :]
    return summed

def attention(q_conv, key_rows, value_cols, doc_ids):
    blocks = SEQ // TOK_DEV
    q_blocks = q_conv.reshape(HEADS, FD, blocks, TOK_DEV).transpose(2, 0, 1, 3)
    k_blocks = key_rows.reshape(HEADS, FD, blocks, TOK_DEV).transpose(2, 0, 1, 3)
    v_blocks = value_cols.reshape(blocks, TOK_DEV, HEADS, HD)
    id_blocks = doc_ids.reshape(blocks, TOK_DEV)

    def advance(carry, block):
        state_in, normer_in, last_id = carry
        q_block, k_block, v_block, id_block = block
        q_feat = features(q_block)
        k_feat = features(k_block)
        carry_mask = (id_block == last_id).astype(jnp.float32)
        result = block_output(q_feat, k_feat, v_block, id_block, carry_mask, state_in, normer_in)
        block_last = id_block[TOK_DEV - 1]
        tail_mask = (id_block == block_last).astype(jnp.float32)
        keep_old = (last_id == block_last).astype(jnp.float32)
        tail_feat = k_feat * tail_mask[None, None, :]
        new_state = keep_old * state_in + jnp.einsum('hfs,shd->hfd', tail_feat, v_block, precision=exact_mode)
        new_normer = keep_old * normer_in + lax.optimization_barrier(jnp.sum(tail_feat, axis=2))
        return ((new_state, new_normer, block_last), result.reshape(TOK_DEV, HEADS * HD))
    start_carry = (jnp.zeros((HEADS, NF, HD), jnp.float32), jnp.zeros((HEADS, NF), jnp.float32), jnp.int32(-1))
    _, outputs = lax.scan(jax.checkpoint(advance), start_carry, (q_blocks, k_blocks, v_blocks, id_blocks))
    return outputs.reshape(SEQ, HEADS * HD)

def reference(queries, keys, values, seg_ids, conv_weight, out_weight, out_grad):
    grad_attn = jnp.dot(out_grad, out_weight.T, preferred_element_type=jnp.float32)
    taps = conv_weight.astype(jnp.float32)

    def forward(query_rows, key_rows, value_cols):
        q_conv = convolve(query_rows, taps, seg_ids)
        return attention(q_conv, key_rows, value_cols, seg_ids)
    _, pullback = jax.vjp(forward, queries.astype(jnp.float32), keys.astype(jnp.float32), values.astype(jnp.float32))
    grad_queries, grad_keys, grad_values = pullback(grad_attn)
    return (grad_queries, grad_keys, grad_values)
```

```python
import jax
import jax.numpy as jnp
from jax import lax
from jax.experimental import pallas as pl
from jax.experimental.pallas import tpu as pltpu
from jax.sharding import PartitionSpec as P

FD = 16


half_root = 0.7071067811865476
split_mode = lax.Precision.HIGH


def entering(shard, axis, combine, identity, reverse):
    size, here = (lax.axis_size(axis), lax.axis_index(axis))
    everything = jax.tree.map(lambda part: lax.all_gather(part, axis), shard)
    start = jax.tree.map(
        lambda part, zero: jnp.broadcast_to(jnp.asarray(zero, part.dtype), part.shape),
        shard,
        identity,
    )

    def step(k, before):
        at = size - 1 - k if reverse else k
        reached = at > here if reverse else at < here
        new = combine(before, jax.tree.map(lambda part: part[at], everything))
        return jax.tree.map(lambda a, b: jnp.where(reached, a, b), new, before)

    return lax.fori_loop(0, size, step, start)


def features(entries):
    scaled = entries * 0.5
    cross = [
        scaled[..., i : i + 1, :] * scaled[..., i + 1 :, :] for i in range(scaled.shape[-2] - 1)
    ]
    return jnp.concatenate(
        [jnp.ones_like(scaled[..., :1, :]), scaled, scaled * scaled * half_root] + cross, axis=-2
    )


def block_output(q_feat, k_feat, head_values, doc_ids, carry_mask, state_in, normer_in):
    length = doc_ids.shape[0]
    causal = jnp.arange(length)[:, None] >= jnp.arange(length)[None, :]
    allowed = (causal & (doc_ids[:, None] == doc_ids[None, :])).astype(jnp.float32)
    scores = jnp.einsum("hft,hfs->hts", q_feat, k_feat, precision=split_mode) * allowed[None, :, :]
    numerator = jnp.einsum("hts,shd->thd", scores, head_values, precision=split_mode)
    numerator = numerator + carry_mask[:, None, None] * jnp.einsum(
        "hft,hfd->thd", q_feat, state_in, precision=split_mode
    )
    denominator = jnp.sum(scores, axis=2).T + carry_mask[:, None] * jnp.einsum(
        "hft,hf->th", q_feat, normer_in, precision=split_mode
    )
    return numerator / denominator[:, :, None]


def join_forward(earlier, later):
    empty_later = later[0][1] == 0.0
    same_doc = earlier[0][1] == later[0][1]
    state_out = jnp.where(empty_later, earlier[2], later[2] + jnp.where(same_doc, earlier[2], 0.0))
    normer_out = jnp.where(empty_later, earlier[3], later[3] + jnp.where(same_doc, earlier[3], 0.0))
    return (
        jnp.where(empty_later, earlier[0], later[0]),
        jnp.where(empty_later, earlier[1], later[1]),
        state_out,
        normer_out,
    )


def join_backward(earlier, later):
    empty_later = later[0][0] == 0.0
    same_doc = earlier[0][0] == later[0][0]
    state_out = jnp.where(empty_later, earlier[2], later[2] + jnp.where(same_doc, earlier[2], 0.0))
    normer_out = jnp.where(empty_later, earlier[3], later[3] + jnp.where(same_doc, earlier[3], 0.0))
    return (
        jnp.where(empty_later, earlier[0], later[0]),
        jnp.where(empty_later, earlier[1], later[1]),
        state_out,
        normer_out,
    )


def body(queries, keys, values, seg_ids, conv_weight, out_weight, out_grad):
    local_heads = queries.shape[0] // FD
    length = queries.shape[1]
    head_width = values.shape[1] // local_heads
    grad_attn = lax.dot_general(
        lax.all_gather(out_grad, "head", axis=1, tiled=True),
        out_weight,
        (((1,), (1,)), ((), ())),
        preferred_element_type=jnp.float32,
    )
    doc_ids = (seg_ids + 1).astype(jnp.float32)
    query_rows = queries.astype(jnp.float32)
    key_heads = keys.astype(jnp.float32).reshape(local_heads, FD, length)
    head_values = values.astype(jnp.float32).reshape(length, local_heads, head_width)
    taps = conv_weight.astype(jnp.float32)
    k_feat, feature_pullback = jax.vjp(features, key_heads)
    tail_mask = (doc_ids == doc_ids[length - 1]).astype(jnp.float32)
    tail_feat = k_feat * tail_mask[None, None, :]
    tail_state = jnp.einsum("hfs,shd->hfd", tail_feat, head_values, precision=split_mode)
    tail_normer = jnp.sum(tail_feat, axis=2)
    forward_piece = (doc_ids[length - 2 :], query_rows[:, length - 2 :], tail_state, tail_normer)
    before = entering(
        forward_piece, "ctx", join_forward, jax.tree.map(jnp.zeros_like, forward_piece), False
    )
    query_ext = jnp.concatenate([before[1], query_rows], axis=1)
    ids_before = jnp.concatenate([before[0], doc_ids])
    q_conv = taps[0][:, None] * query_rows
    for offset in (1, 2):
        same_doc = (ids_before[2 - offset : 2 - offset + length] == doc_ids).astype(jnp.float32)
        q_conv = (
            q_conv
            + taps[offset][:, None]
            * query_ext[:, 2 - offset : 2 - offset + length]
            * same_doc[None, :]
        )
    carry_mask = (doc_ids == before[0][1]).astype(jnp.float32)

    def local_forward(q_conv_in, k_feat_in, values_in, state_in, normer_in):
        q_feat = features(q_conv_in.reshape(local_heads, FD, length))
        result = block_output(
            q_feat, k_feat_in, values_in, doc_ids, carry_mask, state_in, normer_in
        )
        return result.reshape(length, local_heads * head_width)

    _, local_pullback = jax.vjp(local_forward, q_conv, k_feat, head_values, before[2], before[3])
    grad_qconv, grad_kfeat, grad_heads, grad_state, grad_normer = local_pullback(grad_attn)
    backward_piece = (doc_ids[:2], grad_qconv[:, :2], grad_state, grad_normer)
    after = entering(
        backward_piece, "ctx", join_backward, jax.tree.map(jnp.zeros_like, backward_piece), True
    )
    head_mask = (doc_ids == after[0][0]).astype(jnp.float32)
    flowing = (
        jnp.einsum("hfd,shd->hfs", after[2], head_values, precision=split_mode)
        + after[3][:, :, None]
    )
    grad_kfeat = grad_kfeat + flowing * head_mask[None, None, :]
    grad_heads = grad_heads + jnp.einsum(
        "hfs,hfd->shd", k_feat * head_mask[None, None, :], after[2], precision=split_mode
    )
    (grad_key_heads,) = feature_pullback(grad_kfeat)
    grad_ext = jnp.concatenate([grad_qconv, after[1]], axis=1)
    ids_after = jnp.concatenate([doc_ids, after[0]])
    grad_queries = taps[0][:, None] * grad_qconv
    for offset in (1, 2):
        same_doc = (ids_after[offset : offset + length] == doc_ids).astype(jnp.float32)
        grad_queries = (
            grad_queries
            + taps[offset][:, None] * grad_ext[:, offset : offset + length] * same_doc[None, :]
        )
    grad_keys = grad_key_heads.reshape(local_heads * FD, length)
    grad_values = grad_heads.reshape(length, local_heads * head_width)
    return (grad_queries, grad_keys, grad_values)


f32, bf16 = jnp.float32, jnp.bfloat16
NN = (((1,), (0,)), ((), ()))
NT = (((1,), (1,)), ((), ()))
TN = (((0,), (0,)), ((), ()))
BLOCKS = 2
SEG_ROW = 2 * FD
V_ROW = 3 * FD


def split(x):
    high = x.astype(bf16)
    return high, (x - high.astype(f32)).astype(bf16)


def dot(a, b, dims):
    return lax.dot_general(a, b, dims, preferred_element_type=f32)


def dot3(a, b, dims):
    return dot(a[0], b[0], dims) + dot(a[0], b[1], dims) + dot(a[1], b[0], dims)


def ahead(x, d):
    return pltpu.roll(x, FD - d, 0)


def phi(u):
    rows = [u, u * u * half_root]
    for d in range(1, FD // 2):
        rows.append(u * ahead(u, d))
    half = FD // 2
    one = (lax.broadcasted_iota(jnp.int32, (half, u.shape[1]), 0) == 0).astype(f32)
    rows.append(jnp.concatenate([u[:half] * u[half:], one], axis=0))
    return jnp.concatenate(rows, axis=0)


def phi_pullback(u, grad):
    total = grad[:FD] + (2.0 * half_root) * u * grad[FD : 2 * FD]
    for d in range(1, FD // 2):
        part = grad[(d + 1) * FD : (d + 2) * FD]
        total = total + part * ahead(u, d) + pltpu.roll(part * u, d, 0)
    half = FD // 2
    last = grad[(half + 1) * FD : (half + 1) * FD + half]
    return total + jnp.concatenate([last * u[half:], last * u[:half]], axis=0)


def head_kernel(pk_ref, g_ref, meta_ref, taps_ref, out_ref, u_ref, du_ref, gext_ref):
    blocks, width = pk_ref.shape[0], pk_ref.shape[2]
    channels = g_ref.shape[1]
    ext = channels + FD
    seq = blocks * width
    size = BLOCKS * width
    chunks = blocks // BLOCKS
    nf = (FD // 2 + 2) * FD

    def load(ref, i, start, rows):
        parts = [ref[i * BLOCKS + j, start : start + rows, :] for j in range(BLOCKS)]
        return jnp.concatenate(parts, axis=1)

    def store(i, start, x, add):
        for j in range(BLOCKS):
            part = x[:, j * width : (j + 1) * width]
            rows = pl.ds(start, x.shape[0])
            if add:
                part = part + out_ref[i * BLOCKS + j, rows, :]
            out_ref[i * BLOCKS + j, rows, :] = part

    raw = jnp.concatenate([pk_ref[j, 0:FD, :].astype(f32) for j in range(blocks)], axis=1) * 0.5
    u_ref[...] = (
        taps_ref[:, 0:1] * raw
        + taps_ref[:, 1:2] * pltpu.roll(raw, 1, 1) * meta_ref[4:5, :]
        + taps_ref[:, 2:3] * pltpu.roll(raw, 2, 1) * meta_ref[5:6, :]
    )
    causal = lax.broadcasted_iota(jnp.int32, (size, size), 0) <= lax.broadcasted_iota(
        jnp.int32, (size, size), 1
    )
    ones_rows = (lax.broadcasted_iota(jnp.int32, (FD, size), 0) == 0).astype(bf16)

    def value_rows(i):
        return jnp.concatenate([load(pk_ref, i, V_ROW, channels), ones_rows], axis=0)

    def forward(i, state):
        span = pl.ds(pl.multiple_of(i * size, size), size)
        u = u_ref[:, span]
        w16 = load(pk_ref, i, FD, FD) * jnp.asarray(0.5, bf16)
        w = w16.astype(f32)
        vext = value_rows(i)
        g = load(g_ref, i, 0, channels)
        seg = meta_ref[0:1, span]
        carry = meta_ref[1:2, span]
        tail = meta_ref[2:3, span]
        keep = meta_ref[3:4, span][:, 0:1]
        seg_t = jnp.broadcast_to(seg, (size, size))
        allowed = jnp.where(causal & (seg_t == seg_t.T), 1.0, 0.0)
        us = split(u)
        x = dot(jnp.concatenate([w16, w16], axis=0), jnp.concatenate(us, axis=0), TN)
        slope = allowed * (1.0 + x)
        p = split(allowed * (1.0 + x + 0.5 * x * x))
        feat_q = split(phi(u) * carry)
        states = split(state)
        numer = dot(vext, p[0], NN) + dot(vext, p[1], NN) + dot3(states, feat_q, NN)
        inverse = 1.0 / numer[channels : channels + 1]
        gp = g * inverse
        dden = -jnp.sum(gp * numer[:channels], axis=0, keepdims=True) * inverse
        gext = jnp.concatenate([gp, dden, jnp.zeros((FD - 1, size), f32)], axis=0)
        gext_ref[:, span] = gext
        gs = split(gext)
        dx = split(slope * (dot(vext, gs[0], TN) + dot(vext, gs[1], TN)))
        du = dot(w16, dx[0], NN) + dot(w16, dx[1], NN)
        dw = dot3(us, dx, NT)
        dv = dot3((gs[0][:channels], gs[1][:channels]), p, NT)
        du_ref[:, span] = du + phi_pullback(u, dot3(states, gs, TN) * carry)
        store(i, channels + FD, dw, False)
        store(i, 0, dv, False)
        feat_k = split(phi(w) * tail)
        return keep * state + dot(vext, feat_k[0], NT) + dot(vext, feat_k[1], NT)

    lax.fori_loop(0, chunks, forward, jnp.zeros((ext, nf), f32))

    def backward(step, adjoint):
        i = chunks - 1 - step
        span = pl.ds(pl.multiple_of(i * size, size), size)
        w = (load(pk_ref, i, FD, FD) * jnp.asarray(0.5, bf16)).astype(f32)
        vext = value_rows(i)
        tail = meta_ref[2:3, span]
        keep = meta_ref[3:4, span][:, 0:1]
        adj = split(adjoint)
        feat_k = split(phi(w) * tail)
        dfeat = (dot(adj[0], vext, TN) + dot(adj[1], vext, TN)) * tail
        old = load(out_ref, i, channels + FD, FD)
        store(i, channels + FD, 0.5 * (old + phi_pullback(w, dfeat)), False)
        store(i, 0, dot3((adj[0][:channels], adj[1][:channels]), feat_k, NN), True)
        feat_q = split(phi(u_ref[:, span]) * meta_ref[1:2, span])
        return keep * adjoint + dot3(split(gext_ref[:, span]), feat_q, NT)

    lax.fori_loop(0, chunks, backward, jnp.zeros((ext, nf), f32))
    du = du_ref[...] * 0.5
    dq = (
        taps_ref[:, 0:1] * du
        + taps_ref[:, 1:2] * pltpu.roll(du, seq - 1, 1) * meta_ref[6:7, :]
        + taps_ref[:, 2:3] * pltpu.roll(du, seq - 2, 1) * meta_ref[7:8, :]
    )
    for j in range(blocks):
        out_ref[j, channels : channels + FD, :] = dq[:, j * width : (j + 1) * width]


def head_call(pk, g, meta, taps):
    blocks, _, width = pk.shape
    channels = g.shape[1]
    return pl.pallas_call(
        head_kernel,
        out_shape=jax.ShapeDtypeStruct((blocks, channels + 2 * FD, width), f32),
        in_specs=[pl.BlockSpec(memory_space=pltpu.VMEM)] * 4,
        out_specs=pl.BlockSpec(memory_space=pltpu.VMEM),
        scratch_shapes=[
            pltpu.VMEM((FD, blocks * width), f32),
            pltpu.VMEM((FD, blocks * width), f32),
            pltpu.VMEM((channels + FD, blocks * width), f32),
        ],
        compiler_params=pltpu.CompilerParams(vmem_limit_bytes=40 * 2**20),
    )(pk, g, meta, taps)


def meta_rows(pk):
    blocks, _, width = pk.shape
    size = BLOCKS * width
    seg = pk[:, SEG_ROW, :].astype(f32).reshape(-1)
    last = jnp.repeat(seg[size - 1 :: size], size)
    before = jnp.concatenate([jnp.full((size,), -1.0, f32), last[:-size]])
    same = lambda a, b: (a == b).astype(f32)
    late = lambda d: same(jnp.pad(seg, (d, 0), constant_values=-1.0)[:-d], seg)
    soon = lambda d: same(jnp.pad(seg, (0, d), constant_values=-1.0)[d:], seg)
    rows = [seg, same(seg, before), same(seg, last), same(before, last)]
    return jnp.stack(rows + [late(1), late(2), soon(1), soon(2)])


def pack(queries, keys, values, seg_ids, size):
    heads, length = queries.shape[0] // FD, queries.shape[1]
    share = size // heads
    twice = lambda x: jnp.repeat(x.reshape(heads, FD, length), share, axis=0)
    seg = jnp.broadcast_to(seg_ids.astype(bf16), (size, FD, length))
    rows = values.T.reshape(size, -1, length)
    return jnp.concatenate([twice(queries), twice(keys), seg, rows], axis=1)


def by_heads(queries, keys, values, seg_ids, conv_weight, out_weight, out_grad):
    size = lax.axis_size("ctx")
    heads, length = queries.shape[0] // FD, queries.shape[1]
    share = size // heads
    swap = lambda x: lax.all_to_all(x, "ctx", 0, 0)
    pk = swap(pack(queries, keys, values, seg_ids, size))
    grad_attn = lax.dot_general(out_weight, out_grad, NT, preferred_element_type=f32)
    g = swap(grad_attn.reshape(size, -1, length))
    head = lax.axis_index("ctx") // share
    taps = lax.dynamic_slice_in_dim(conv_weight.astype(f32).T, head * FD, FD, 0)
    taps = jnp.pad(taps, ((0, 0), (0, 128 - taps.shape[1])))
    out = swap(head_call(pk, g, meta_rows(pk), taps))
    channels = g.shape[1]
    joined = lambda x: x.reshape(heads, share, FD, length).sum(1).reshape(heads * FD, length)
    grad_values = out[:, :channels].reshape(-1, length).T
    return (
        joined(out[:, channels : channels + FD]),
        joined(out[:, channels + FD :]),
        grad_values,
    )


def solution(mesh):
    in_specs = (
        P("head", "ctx"),
        P("head", "ctx"),
        P("ctx", "head"),
        P("ctx"),
        P(None, "head"),
        P("head", None),
        P("ctx", "head"),
    )
    out_specs = (P("head", "ctx"), P("head", "ctx"), P("ctx", "head"))

    def program(queries, *rest):
        heads = queries.shape[0] // FD
        spread = mesh.shape["head"] == 1 and mesh.shape["ctx"] == 2 * heads
        inner = by_heads if spread else body
        return jax.shard_map(
            inner, mesh=mesh, in_specs=in_specs, out_specs=out_specs, check_vma=False
        )(queries, *rest)

    return program
```

```python
import jax
import jax.numpy as jnp
from jax import lax
from jax.experimental import pallas as pl
from jax.experimental.pallas import tpu as pltpu
from jax.sharding import PartitionSpec as P

FD = 16


half_root = 0.7071067811865476
split_mode = lax.Precision.HIGH


def entering(shard, axis, combine, identity, reverse):
    size, here = (lax.axis_size(axis), lax.axis_index(axis))
    everything = jax.tree.map(lambda part: lax.all_gather(part, axis), shard)
    start = jax.tree.map(
        lambda part, zero: jnp.broadcast_to(jnp.asarray(zero, part.dtype), part.shape),
        shard,
        identity,
    )

    def step(k, before):
        at = size - 1 - k if reverse else k
        reached = at > here if reverse else at < here
        new = combine(before, jax.tree.map(lambda part: part[at], everything))
        return jax.tree.map(lambda a, b: jnp.where(reached, a, b), new, before)

    return lax.fori_loop(0, size, step, start)


def features(entries):
    scaled = entries * 0.5
    cross = [
        scaled[..., i : i + 1, :] * scaled[..., i + 1 :, :] for i in range(scaled.shape[-2] - 1)
    ]
    return jnp.concatenate(
        [jnp.ones_like(scaled[..., :1, :]), scaled, scaled * scaled * half_root] + cross, axis=-2
    )


def block_output(q_feat, k_feat, head_values, doc_ids, carry_mask, state_in, normer_in):
    length = doc_ids.shape[0]
    causal = jnp.arange(length)[:, None] >= jnp.arange(length)[None, :]
    allowed = (causal & (doc_ids[:, None] == doc_ids[None, :])).astype(jnp.float32)
    scores = jnp.einsum("hft,hfs->hts", q_feat, k_feat, precision=split_mode) * allowed[None, :, :]
    numerator = jnp.einsum("hts,shd->thd", scores, head_values, precision=split_mode)
    numerator = numerator + carry_mask[:, None, None] * jnp.einsum(
        "hft,hfd->thd", q_feat, state_in, precision=split_mode
    )
    denominator = jnp.sum(scores, axis=2).T + carry_mask[:, None] * jnp.einsum(
        "hft,hf->th", q_feat, normer_in, precision=split_mode
    )
    return numerator / denominator[:, :, None]


def join_forward(earlier, later):
    empty_later = later[0][1] == 0.0
    same_doc = earlier[0][1] == later[0][1]
    state_out = jnp.where(empty_later, earlier[2], later[2] + jnp.where(same_doc, earlier[2], 0.0))
    normer_out = jnp.where(empty_later, earlier[3], later[3] + jnp.where(same_doc, earlier[3], 0.0))
    return (
        jnp.where(empty_later, earlier[0], later[0]),
        jnp.where(empty_later, earlier[1], later[1]),
        state_out,
        normer_out,
    )


def join_backward(earlier, later):
    empty_later = later[0][0] == 0.0
    same_doc = earlier[0][0] == later[0][0]
    state_out = jnp.where(empty_later, earlier[2], later[2] + jnp.where(same_doc, earlier[2], 0.0))
    normer_out = jnp.where(empty_later, earlier[3], later[3] + jnp.where(same_doc, earlier[3], 0.0))
    return (
        jnp.where(empty_later, earlier[0], later[0]),
        jnp.where(empty_later, earlier[1], later[1]),
        state_out,
        normer_out,
    )


def body(queries, keys, values, seg_ids, conv_weight, out_weight, out_grad):
    local_heads = queries.shape[0] // FD
    length = queries.shape[1]
    head_width = values.shape[1] // local_heads
    grad_attn = lax.dot_general(
        lax.all_gather(out_grad, "head", axis=1, tiled=True),
        out_weight,
        (((1,), (1,)), ((), ())),
        preferred_element_type=jnp.float32,
    )
    doc_ids = (seg_ids + 1).astype(jnp.float32)
    query_rows = queries.astype(jnp.float32)
    key_heads = keys.astype(jnp.float32).reshape(local_heads, FD, length)
    head_values = values.astype(jnp.float32).reshape(length, local_heads, head_width)
    taps = conv_weight.astype(jnp.float32)
    k_feat, feature_pullback = jax.vjp(features, key_heads)
    tail_mask = (doc_ids == doc_ids[length - 1]).astype(jnp.float32)
    tail_feat = k_feat * tail_mask[None, None, :]
    tail_state = jnp.einsum("hfs,shd->hfd", tail_feat, head_values, precision=split_mode)
    tail_normer = jnp.sum(tail_feat, axis=2)
    forward_piece = (doc_ids[length - 2 :], query_rows[:, length - 2 :], tail_state, tail_normer)
    before = entering(
        forward_piece, "ctx", join_forward, jax.tree.map(jnp.zeros_like, forward_piece), False
    )
    query_ext = jnp.concatenate([before[1], query_rows], axis=1)
    ids_before = jnp.concatenate([before[0], doc_ids])
    q_conv = taps[0][:, None] * query_rows
    for offset in (1, 2):
        same_doc = (ids_before[2 - offset : 2 - offset + length] == doc_ids).astype(jnp.float32)
        q_conv = (
            q_conv
            + taps[offset][:, None]
            * query_ext[:, 2 - offset : 2 - offset + length]
            * same_doc[None, :]
        )
    carry_mask = (doc_ids == before[0][1]).astype(jnp.float32)

    def local_forward(q_conv_in, k_feat_in, values_in, state_in, normer_in):
        q_feat = features(q_conv_in.reshape(local_heads, FD, length))
        result = block_output(
            q_feat, k_feat_in, values_in, doc_ids, carry_mask, state_in, normer_in
        )
        return result.reshape(length, local_heads * head_width)

    _, local_pullback = jax.vjp(local_forward, q_conv, k_feat, head_values, before[2], before[3])
    grad_qconv, grad_kfeat, grad_heads, grad_state, grad_normer = local_pullback(grad_attn)
    backward_piece = (doc_ids[:2], grad_qconv[:, :2], grad_state, grad_normer)
    after = entering(
        backward_piece, "ctx", join_backward, jax.tree.map(jnp.zeros_like, backward_piece), True
    )
    head_mask = (doc_ids == after[0][0]).astype(jnp.float32)
    flowing = (
        jnp.einsum("hfd,shd->hfs", after[2], head_values, precision=split_mode)
        + after[3][:, :, None]
    )
    grad_kfeat = grad_kfeat + flowing * head_mask[None, None, :]
    grad_heads = grad_heads + jnp.einsum(
        "hfs,hfd->shd", k_feat * head_mask[None, None, :], after[2], precision=split_mode
    )
    (grad_key_heads,) = feature_pullback(grad_kfeat)
    grad_ext = jnp.concatenate([grad_qconv, after[1]], axis=1)
    ids_after = jnp.concatenate([doc_ids, after[0]])
    grad_queries = taps[0][:, None] * grad_qconv
    for offset in (1, 2):
        same_doc = (ids_after[offset : offset + length] == doc_ids).astype(jnp.float32)
        grad_queries = (
            grad_queries
            + taps[offset][:, None] * grad_ext[:, offset : offset + length] * same_doc[None, :]
        )
    grad_keys = grad_key_heads.reshape(local_heads * FD, length)
    grad_values = grad_heads.reshape(length, local_heads * head_width)
    return (grad_queries, grad_keys, grad_values)


f32, bf16 = jnp.float32, jnp.bfloat16
NN = (((1,), (0,)), ((), ()))
NT = (((1,), (1,)), ((), ()))
TN = (((0,), (0,)), ((), ()))
BLOCKS = 2
SEG_ROW = 2 * FD
V_ROW = 3 * FD


def split(x):
    high = x.astype(bf16)
    return high, (x - high.astype(f32)).astype(bf16)


def dot(a, b, dims):
    return lax.dot_general(a, b, dims, preferred_element_type=f32)


def dot3(a, b, dims):
    return dot(a[0], b[0], dims) + dot(a[0], b[1], dims) + dot(a[1], b[0], dims)


def ahead(x, d):
    return pltpu.roll(x, FD - d, 0)


def phi(u):
    rows = [u, u * u * half_root]
    for d in range(1, FD // 2):
        rows.append(u * ahead(u, d))
    half = FD // 2
    one = (lax.broadcasted_iota(jnp.int32, (half, u.shape[1]), 0) == 0).astype(f32)
    rows.append(jnp.concatenate([u[:half] * u[half:], one], axis=0))
    return jnp.concatenate(rows, axis=0)


def phi_pullback(u, grad):
    total = grad[:FD] + (2.0 * half_root) * u * grad[FD : 2 * FD]
    for d in range(1, FD // 2):
        part = grad[(d + 1) * FD : (d + 2) * FD]
        total = total + part * ahead(u, d) + pltpu.roll(part * u, d, 0)
    half = FD // 2
    last = grad[(half + 1) * FD : (half + 1) * FD + half]
    return total + jnp.concatenate([last * u[half:], last * u[:half]], axis=0)


def load(ref, i, start, rows):
    parts = [ref[i * BLOCKS + j, start : start + rows, :] for j in range(BLOCKS)]
    return jnp.concatenate(parts, axis=1)


def store(ref, i, start, x):
    width = ref.shape[2]
    for j in range(BLOCKS):
        ref[i * BLOCKS + j, start : start + x.shape[0], :] = x[:, j * width : (j + 1) * width]


def key_rows(pk_ref, i):
    return load(pk_ref, i, FD, FD) * jnp.asarray(0.5, bf16)


def value_rows(pk_ref, i):
    channels = pk_ref.shape[1] - V_ROW
    values = load(pk_ref, i, V_ROW, channels)
    ones = lax.broadcasted_iota(jnp.int32, (FD, values.shape[1]), 0) == 0
    return jnp.concatenate([values, ones.astype(bf16)], axis=0)


def lanes(i, size):
    return pl.ds(pl.multiple_of(i * size, size), size)


def ending_kernel(pk_ref, meta_ref, state_ref):
    size = BLOCKS * pk_ref.shape[2]

    def step(i, state):
        tail = meta_ref[8:9, lanes(i, size)]
        feat_k = split(phi(key_rows(pk_ref, i).astype(f32)) * tail)
        vext = value_rows(pk_ref, i)
        return state + dot(vext, feat_k[0], NT) + dot(vext, feat_k[1], NT)

    start = jnp.zeros(state_ref.shape, f32)
    state_ref[...] = lax.fori_loop(0, pk_ref.shape[0] // BLOCKS, step, start)


def forward_kernel(
    pk_ref, g_ref, meta_ref, taps_ref, edge_ref, state_ref, part_ref, du_ref, inc_ref, pay_ref, u_ref
):
    blocks, width = pk_ref.shape[0], pk_ref.shape[2]
    channels = g_ref.shape[1]
    ext, nf = state_ref.shape
    size = BLOCKS * width

    raw = [pk_ref[j, 0:FD, :].astype(f32) for j in range(blocks)]
    raw = jnp.concatenate([edge_ref[...].astype(f32)] + raw, axis=1) * 0.5
    u_ref[...] = (
        taps_ref[:, 0:1] * raw[:, width:]
        + taps_ref[:, 1:2] * pltpu.roll(raw, 1, 1)[:, width:] * meta_ref[4:5, :]
        + taps_ref[:, 2:3] * pltpu.roll(raw, 2, 1)[:, width:] * meta_ref[5:6, :]
    )
    causal = lax.broadcasted_iota(jnp.int32, (size, size), 0) <= lax.broadcasted_iota(
        jnp.int32, (size, size), 1
    )

    def step(i, carried):
        state, leading = carried
        span = lanes(i, size)
        u = u_ref[:, span]
        w16 = key_rows(pk_ref, i)
        vext = value_rows(pk_ref, i)
        g = load(g_ref, i, 0, channels)
        seg = meta_ref[0:1, span]
        carry = meta_ref[1:2, span]
        tail = meta_ref[2:3, span]
        keep = meta_ref[3:4, span][:, 0:1]
        first = meta_ref[9:10, span][:, 0:1]
        seg_t = jnp.broadcast_to(seg, (size, size))
        allowed = jnp.where(causal & (seg_t == seg_t.T), 1.0, 0.0)
        us = split(u)
        x = dot(jnp.concatenate([w16, w16], axis=0), jnp.concatenate(us, axis=0), TN)
        slope = allowed * (1.0 + x)
        p = split(allowed * (1.0 + x + 0.5 * x * x))
        feat_q = split(phi(u) * carry)
        states = split(state)
        numer = dot(vext, p[0], NN) + dot(vext, p[1], NN) + dot3(states, feat_q, NN)
        inverse = 1.0 / numer[channels : channels + 1]
        gp = g * inverse
        dden = -jnp.sum(gp * numer[:channels], axis=0, keepdims=True) * inverse
        gext = jnp.concatenate([gp, dden, jnp.zeros((FD - 1, size), f32)], axis=0)
        gs = split(gext)
        dx = split(slope * (dot(vext, gs[0], TN) + dot(vext, gs[1], TN)))
        du = dot(w16, dx[0], NN) + dot(w16, dx[1], NN)
        dw = dot3(us, dx, NT)
        dv = dot3((gs[0][:channels], gs[1][:channels]), p, NT)
        du_ref[:, span] = du + phi_pullback(u, dot3(states, gs, TN) * carry)
        store(part_ref, i, 0, dv)
        store(part_ref, i, channels, dw)
        inc = dot3(gs, feat_q, NT)
        inc_ref[i] = inc
        feat_k = split(phi(key_rows(pk_ref, i).astype(f32)) * tail)
        state = keep * state + dot(vext, feat_k[0], NT) + dot(vext, feat_k[1], NT)
        return state, leading + first * inc

    start = (state_ref[...], jnp.zeros((ext, nf), f32))
    _, leading = lax.fori_loop(0, blocks // BLOCKS, step, start)
    pay_ref[0:ext, :] = leading
    pay_ref[ext : ext + FD, :] = jnp.zeros((FD, nf), f32)
    pay_ref[ext : ext + FD, 0:width] = du_ref[:, 0:width]


def backward_kernel(pk_ref, meta_ref, taps_ref, part_ref, du_ref, inc_ref, pay_ref, out_ref):
    blocks, width = pk_ref.shape[0], pk_ref.shape[2]
    ext, nf = inc_ref.shape[1:]
    channels = ext - FD
    size = BLOCKS * width
    chunks = blocks // BLOCKS

    def step(count, adjoint):
        i = chunks - 1 - count
        span = lanes(i, size)
        w = key_rows(pk_ref, i).astype(f32)
        vext = value_rows(pk_ref, i)
        tail = meta_ref[2:3, span]
        keep = meta_ref[3:4, span][:, 0:1]
        adj = split(adjoint)
        feat_k = split(phi(w) * tail)
        dfeat = (dot(adj[0], vext, TN) + dot(adj[1], vext, TN)) * tail
        dw = load(part_ref, i, channels, FD) + phi_pullback(w, dfeat)
        store(out_ref, i, channels + FD, 0.5 * dw)
        dv = dot3((adj[0][:channels], adj[1][:channels]), feat_k, NN)
        store(out_ref, i, 0, load(part_ref, i, 0, channels) + dv)
        return keep * adjoint + inc_ref[i]

    lax.fori_loop(0, chunks, step, pay_ref[0:ext, :])
    du = jnp.concatenate([du_ref[...], pay_ref[ext : ext + FD, 0:width]], axis=1) * 0.5
    seq, total = blocks * width, (blocks + 1) * width
    dq = (
        taps_ref[:, 0:1] * du[:, :seq]
        + taps_ref[:, 1:2] * pltpu.roll(du, total - 1, 1)[:, :seq] * meta_ref[6:7, :]
        + taps_ref[:, 2:3] * pltpu.roll(du, total - 2, 1)[:, :seq] * meta_ref[7:8, :]
    )
    for j in range(blocks):
        out_ref[j, channels : channels + FD, :] = dq[:, j * width : (j + 1) * width]


def call(kernel, args, outs, scratch=(), flops=0):
    shapes = [jax.ShapeDtypeStruct(shape, f32) for shape in outs]
    return pl.pallas_call(
        kernel,
        out_shape=shapes,
        in_specs=[pl.BlockSpec(memory_space=pltpu.VMEM)] * len(args),
        out_specs=[pl.BlockSpec(memory_space=pltpu.VMEM)] * len(outs),
        scratch_shapes=[pltpu.VMEM(shape, f32) for shape in scratch],
        compiler_params=pltpu.CompilerParams(vmem_limit_bytes=40 * 2**20),
        cost_estimate=pl.CostEstimate(flops=flops, bytes_accessed=2**21, transcendentals=0),
    )(*args)


def meta_rows(pk, edge_before, edge_after):
    width = pk.shape[2]
    size = BLOCKS * width
    seg = pk[:, SEG_ROW, :].astype(f32).reshape(-1)
    earlier = edge_before[SEG_ROW].astype(f32)
    later = edge_after[SEG_ROW].astype(f32)
    last = jnp.repeat(seg[size - 1 :: size], size)
    open_here = earlier[width - 1]
    before = jnp.concatenate([jnp.full((size,), open_here), last[:-size]])
    same = lambda a, b: (a == b).astype(f32)
    late = lambda d: same(jnp.concatenate([earlier[width - d :], seg[:-d]]), seg)
    soon = lambda d: same(jnp.concatenate([seg[d:], later[:d]]), seg)
    rows = [seg, same(seg, before), same(seg, last), same(before, last)]
    rows += [late(1), late(2), soon(1), soon(2)]
    rows += [same(seg, seg[-1]), same(before, open_here)]
    return jnp.pad(jnp.stack(rows), ((0, 6), (0, 0)))


def pack(queries, keys, values, seg_ids):
    heads, length = queries.shape[0] // FD, queries.shape[1]
    shaped = lambda x: x.reshape(heads, -1, length)
    seg = jnp.broadcast_to((seg_ids + 1).astype(bf16), (heads, FD, length))
    return jnp.concatenate([shaped(queries), shaped(keys), seg, shaped(values.T)], axis=1)


def by_heads(queries, keys, values, seg_ids, conv_weight, out_weight, out_grad):
    heads, length = queries.shape[0] // FD, queries.shape[1]
    groups = [[half * heads + h for h in range(heads)] for half in (0, 1)]
    swap = lambda x: lax.all_to_all(x, "ctx", 0, 0, axis_index_groups=groups)
    onward = lambda x: lax.ppermute(x, "ctx", [(h, h + heads) for h in range(heads)])
    back = lambda x: lax.ppermute(x, "ctx", [(h + heads, h) for h in range(heads)])
    pk = swap(pack(queries, keys, values, seg_ids))
    grad_attn = lax.dot_general(out_weight, out_grad, NT, preferred_element_type=f32)
    g = swap(grad_attn.reshape(heads, -1, length))
    channels = g.shape[1]
    head = lax.rem(lax.axis_index("ctx"), heads)
    taps = lax.dynamic_slice_in_dim(conv_weight.astype(f32).T, head * FD, FD, 0)
    taps = jnp.pad(taps, ((0, 0), (0, 128 - taps.shape[1])))
    edge_before = onward(pk[-1, :V_ROW])
    edge_after = back(pk[0, :V_ROW])
    meta = meta_rows(pk, edge_before, edge_after)
    ext, nf = channels + FD, (FD // 2 + 2) * FD
    seq = heads * length
    (ending,) = call(ending_kernel, (pk, meta), [(ext, nf)], flops=4 * ext * nf * seq)
    part, du, inc, pay = call(
        forward_kernel,
        (pk, g, meta, taps, edge_before[:FD], onward(ending)),
        [(heads, ext, length), (FD, seq), (heads // BLOCKS, ext, nf), (ext + FD, nf)],
        [(FD, seq)],
        flops=40 * ext * nf * seq,
    )
    (out,) = call(
        backward_kernel,
        (pk, meta, taps, part, du, inc, back(pay)),
        [(heads, ext + FD, length)],
        flops=10 * ext * nf * seq,
    )
    out = swap(out)
    return (
        out[:, channels : channels + FD].reshape(heads * FD, length),
        out[:, channels + FD :].reshape(heads * FD, length),
        out[:, :channels].reshape(-1, length).T,
    )


def solution(mesh):
    in_specs = (
        P("head", "ctx"),
        P("head", "ctx"),
        P("ctx", "head"),
        P("ctx"),
        P(None, "head"),
        P("head", None),
        P("ctx", "head"),
    )
    out_specs = (P("head", "ctx"), P("head", "ctx"), P("ctx", "head"))

    def program(queries, *rest):
        heads = queries.shape[0] // FD
        spread = mesh.shape["head"] == 1 and mesh.shape["ctx"] == 2 * heads
        inner = by_heads if spread else body
        return jax.shard_map(
            inner, mesh=mesh, in_specs=in_specs, out_specs=out_specs, check_vma=False
        )(queries, *rest)

    return program
```

```python
import jax
import jax.numpy as jnp
from jax import lax
from jax.experimental import pallas as pl
from jax.experimental.pallas import tpu as pltpu
from jax.sharding import PartitionSpec as P

FD = 16


half_root = 0.7071067811865476
split_mode = lax.Precision.HIGH


def entering(shard, axis, combine, identity, reverse):
    size, here = (lax.axis_size(axis), lax.axis_index(axis))
    everything = jax.tree.map(lambda part: lax.all_gather(part, axis), shard)
    start = jax.tree.map(
        lambda part, zero: jnp.broadcast_to(jnp.asarray(zero, part.dtype), part.shape),
        shard,
        identity,
    )

    def step(k, before):
        at = size - 1 - k if reverse else k
        reached = at > here if reverse else at < here
        new = combine(before, jax.tree.map(lambda part: part[at], everything))
        return jax.tree.map(lambda a, b: jnp.where(reached, a, b), new, before)

    return lax.fori_loop(0, size, step, start)


def features(entries):
    scaled = entries * 0.5
    cross = [
        scaled[..., i : i + 1, :] * scaled[..., i + 1 :, :] for i in range(scaled.shape[-2] - 1)
    ]
    return jnp.concatenate(
        [jnp.ones_like(scaled[..., :1, :]), scaled, scaled * scaled * half_root] + cross, axis=-2
    )


def block_output(q_feat, k_feat, head_values, doc_ids, carry_mask, state_in, normer_in):
    length = doc_ids.shape[0]
    causal = jnp.arange(length)[:, None] >= jnp.arange(length)[None, :]
    allowed = (causal & (doc_ids[:, None] == doc_ids[None, :])).astype(jnp.float32)
    scores = jnp.einsum("hft,hfs->hts", q_feat, k_feat, precision=split_mode) * allowed[None, :, :]
    numerator = jnp.einsum("hts,shd->thd", scores, head_values, precision=split_mode)
    numerator = numerator + carry_mask[:, None, None] * jnp.einsum(
        "hft,hfd->thd", q_feat, state_in, precision=split_mode
    )
    denominator = jnp.sum(scores, axis=2).T + carry_mask[:, None] * jnp.einsum(
        "hft,hf->th", q_feat, normer_in, precision=split_mode
    )
    return numerator / denominator[:, :, None]


def join_forward(earlier, later):
    empty_later = later[0][1] == 0.0
    same_doc = earlier[0][1] == later[0][1]
    state_out = jnp.where(empty_later, earlier[2], later[2] + jnp.where(same_doc, earlier[2], 0.0))
    normer_out = jnp.where(empty_later, earlier[3], later[3] + jnp.where(same_doc, earlier[3], 0.0))
    return (
        jnp.where(empty_later, earlier[0], later[0]),
        jnp.where(empty_later, earlier[1], later[1]),
        state_out,
        normer_out,
    )


def join_backward(earlier, later):
    empty_later = later[0][0] == 0.0
    same_doc = earlier[0][0] == later[0][0]
    state_out = jnp.where(empty_later, earlier[2], later[2] + jnp.where(same_doc, earlier[2], 0.0))
    normer_out = jnp.where(empty_later, earlier[3], later[3] + jnp.where(same_doc, earlier[3], 0.0))
    return (
        jnp.where(empty_later, earlier[0], later[0]),
        jnp.where(empty_later, earlier[1], later[1]),
        state_out,
        normer_out,
    )


def body(queries, keys, values, seg_ids, conv_weight, out_weight, out_grad):
    local_heads = queries.shape[0] // FD
    length = queries.shape[1]
    head_width = values.shape[1] // local_heads
    grad_attn = lax.dot_general(
        lax.all_gather(out_grad, "head", axis=1, tiled=True),
        out_weight,
        (((1,), (1,)), ((), ())),
        preferred_element_type=jnp.float32,
    )
    doc_ids = (seg_ids + 1).astype(jnp.float32)
    query_rows = queries.astype(jnp.float32)
    key_heads = keys.astype(jnp.float32).reshape(local_heads, FD, length)
    head_values = values.astype(jnp.float32).reshape(length, local_heads, head_width)
    taps = conv_weight.astype(jnp.float32)
    k_feat, feature_pullback = jax.vjp(features, key_heads)
    tail_mask = (doc_ids == doc_ids[length - 1]).astype(jnp.float32)
    tail_feat = k_feat * tail_mask[None, None, :]
    tail_state = jnp.einsum("hfs,shd->hfd", tail_feat, head_values, precision=split_mode)
    tail_normer = jnp.sum(tail_feat, axis=2)
    forward_piece = (doc_ids[length - 2 :], query_rows[:, length - 2 :], tail_state, tail_normer)
    before = entering(
        forward_piece, "ctx", join_forward, jax.tree.map(jnp.zeros_like, forward_piece), False
    )
    query_ext = jnp.concatenate([before[1], query_rows], axis=1)
    ids_before = jnp.concatenate([before[0], doc_ids])
    q_conv = taps[0][:, None] * query_rows
    for offset in (1, 2):
        same_doc = (ids_before[2 - offset : 2 - offset + length] == doc_ids).astype(jnp.float32)
        q_conv = (
            q_conv
            + taps[offset][:, None]
            * query_ext[:, 2 - offset : 2 - offset + length]
            * same_doc[None, :]
        )
    carry_mask = (doc_ids == before[0][1]).astype(jnp.float32)

    def local_forward(q_conv_in, k_feat_in, values_in, state_in, normer_in):
        q_feat = features(q_conv_in.reshape(local_heads, FD, length))
        result = block_output(
            q_feat, k_feat_in, values_in, doc_ids, carry_mask, state_in, normer_in
        )
        return result.reshape(length, local_heads * head_width)

    _, local_pullback = jax.vjp(local_forward, q_conv, k_feat, head_values, before[2], before[3])
    grad_qconv, grad_kfeat, grad_heads, grad_state, grad_normer = local_pullback(grad_attn)
    backward_piece = (doc_ids[:2], grad_qconv[:, :2], grad_state, grad_normer)
    after = entering(
        backward_piece, "ctx", join_backward, jax.tree.map(jnp.zeros_like, backward_piece), True
    )
    head_mask = (doc_ids == after[0][0]).astype(jnp.float32)
    flowing = (
        jnp.einsum("hfd,shd->hfs", after[2], head_values, precision=split_mode)
        + after[3][:, :, None]
    )
    grad_kfeat = grad_kfeat + flowing * head_mask[None, None, :]
    grad_heads = grad_heads + jnp.einsum(
        "hfs,hfd->shd", k_feat * head_mask[None, None, :], after[2], precision=split_mode
    )
    (grad_key_heads,) = feature_pullback(grad_kfeat)
    grad_ext = jnp.concatenate([grad_qconv, after[1]], axis=1)
    ids_after = jnp.concatenate([doc_ids, after[0]])
    grad_queries = taps[0][:, None] * grad_qconv
    for offset in (1, 2):
        same_doc = (ids_after[offset : offset + length] == doc_ids).astype(jnp.float32)
        grad_queries = (
            grad_queries
            + taps[offset][:, None] * grad_ext[:, offset : offset + length] * same_doc[None, :]
        )
    grad_keys = grad_key_heads.reshape(local_heads * FD, length)
    grad_values = grad_heads.reshape(length, local_heads * head_width)
    return (grad_queries, grad_keys, grad_values)


f32, bf16 = jnp.float32, jnp.bfloat16
NN = (((1,), (0,)), ((), ()))
NT = (((1,), (1,)), ((), ()))
TN = (((0,), (0,)), ((), ()))
BLOCKS = 2
V_ROW = 2 * FD


def split(x):
    high = x.astype(bf16)
    return high, (x - high.astype(f32)).astype(bf16)


def dot(a, b, dims):
    return lax.dot_general(a, b, dims, preferred_element_type=f32)


def dot3(a, b, dims):
    return dot(a[0], b[0], dims) + dot(a[0], b[1], dims) + dot(a[1], b[0], dims)


def ahead(x, d):
    return pltpu.roll(x, FD - d, 0)


def phi(u):
    rows = [u, u * u * half_root]
    for d in range(1, FD // 2):
        rows.append(u * ahead(u, d))
    half = FD // 2
    one = (lax.broadcasted_iota(jnp.int32, (half, u.shape[1]), 0) == 0).astype(f32)
    rows.append(jnp.concatenate([u[:half] * u[half:], one], axis=0))
    return jnp.concatenate(rows, axis=0)


def phi_pullback(u, grad):
    total = grad[:FD] + (2.0 * half_root) * u * grad[FD : 2 * FD]
    for d in range(1, FD // 2):
        part = grad[(d + 1) * FD : (d + 2) * FD]
        total = total + part * ahead(u, d) + pltpu.roll(part * u, d, 0)
    half = FD // 2
    last = grad[(half + 1) * FD : (half + 1) * FD + half]
    return total + jnp.concatenate([last * u[half:], last * u[:half]], axis=0)


def load(ref, i, start, rows):
    parts = [ref[i * BLOCKS + j, start : start + rows, :] for j in range(BLOCKS)]
    return jnp.concatenate(parts, axis=1)


def store(ref, i, start, x):
    width = ref.shape[2]
    for j in range(BLOCKS):
        ref[i * BLOCKS + j, start : start + x.shape[0], :] = x[:, j * width : (j + 1) * width]


def key_rows(pk_ref, i):
    return load(pk_ref, i, FD, FD) * jnp.asarray(0.5, bf16)


def value_rows(pk_ref, i):
    channels = pk_ref.shape[1] - V_ROW
    values = load(pk_ref, i, V_ROW, channels)
    ones = lax.broadcasted_iota(jnp.int32, (FD, values.shape[1]), 0) == 0
    return jnp.concatenate([values, ones.astype(bf16)], axis=0)


def lanes(i, size):
    return pl.ds(pl.multiple_of(i * size, size), size)


def ending_kernel(pk_ref, meta_ref, state_ref):
    size = BLOCKS * pk_ref.shape[2]

    def step(i, state):
        tail = meta_ref[8:9, lanes(i, size)]
        feat_k = split(phi(key_rows(pk_ref, i).astype(f32)) * tail)
        vext = value_rows(pk_ref, i)
        return state + dot(vext, feat_k[0], NT) + dot(vext, feat_k[1], NT)

    blocks, width = pk_ref.shape[0], pk_ref.shape[2]
    ext, nf = state_ref.shape[0] - FD, state_ref.shape[1]
    state_ref[0:ext, :] = lax.fori_loop(0, blocks // BLOCKS, step, jnp.zeros((ext, nf), f32))
    state_ref[ext : ext + FD, :] = jnp.zeros((FD, nf), f32)
    state_ref[ext : ext + FD, 0:width] = pk_ref[blocks - 1, 0:FD, :].astype(f32)


def attend(pk_ref, meta_ref, u_ref, i):
    size = BLOCKS * pk_ref.shape[2]
    span = lanes(i, size)
    seg_t = jnp.broadcast_to(meta_ref[0:1, span], (size, size))
    causal = lax.broadcasted_iota(jnp.int32, (size, size), 0) <= lax.broadcasted_iota(
        jnp.int32, (size, size), 1
    )
    allowed = jnp.where(causal & (seg_t == seg_t.T), 1.0, 0.0)
    us = split(u_ref[:, span])
    w16 = key_rows(pk_ref, i)
    x = dot(jnp.concatenate([w16, w16], axis=0), jnp.concatenate(us, axis=0), TN)
    return allowed * (1.0 + x), split(allowed * (1.0 + x + 0.5 * x * x))


def query_grad(pk_ref, meta_ref, u_ref, slope, gs, states, i):
    span = lanes(i, BLOCKS * pk_ref.shape[2])
    vext = value_rows(pk_ref, i)
    w16 = key_rows(pk_ref, i)
    dx = split(slope * (dot(vext, gs[0], TN) + dot(vext, gs[1], TN)))
    dfeat = dot3(states, gs, TN) * meta_ref[1:2, span]
    return dx, dot(w16, dx[0], NN) + dot(w16, dx[1], NN) + phi_pullback(u_ref[:, span], dfeat)


def forward_kernel(
    pk_ref, g_ref, meta_ref, taps_ref, state_ref, u_ref, gext_ref, states_ref, inc_ref, pay_ref
):
    blocks, width = pk_ref.shape[0], pk_ref.shape[2]
    channels = g_ref.shape[1]
    ext, nf = channels + FD, state_ref.shape[1]
    size = BLOCKS * width

    raw = [pk_ref[j, 0:FD, :].astype(f32) for j in range(blocks)]
    raw = jnp.concatenate([state_ref[ext : ext + FD, 0:width]] + raw, axis=1) * 0.5
    u_ref[...] = (
        taps_ref[:, 0:1] * raw[:, width:]
        + taps_ref[:, 1:2] * pltpu.roll(raw, 1, 1)[:, width:] * meta_ref[4:5, :]
        + taps_ref[:, 2:3] * pltpu.roll(raw, 2, 1)[:, width:] * meta_ref[5:6, :]
    )

    def step(i, carried):
        state, leading = carried
        span = lanes(i, size)
        vext = value_rows(pk_ref, i)
        keep = meta_ref[3:4, span][:, 0:1]
        first = meta_ref[9:10, span][:, 0:1]
        _, p = attend(pk_ref, meta_ref, u_ref, i)
        feat_q = split(phi(u_ref[:, span]) * meta_ref[1:2, span])
        states_ref[i] = state
        numer = dot(vext, p[0], NN) + dot(vext, p[1], NN) + dot3(split(state), feat_q, NN)
        inverse = 1.0 / numer[channels : channels + 1]
        gp = load(g_ref, i, 0, channels) * inverse
        dden = -jnp.sum(gp * numer[:channels], axis=0, keepdims=True) * inverse
        gext = jnp.concatenate([gp, dden, jnp.zeros((FD - 1, size), f32)], axis=0)
        gext_ref[:, span] = gext
        inc = dot3(split(gext), feat_q, NT)
        inc_ref[i] = inc
        feat_k = split(phi(key_rows(pk_ref, i).astype(f32)) * meta_ref[2:3, span])
        state = keep * state + dot(vext, feat_k[0], NT) + dot(vext, feat_k[1], NT)
        return state, leading + first * inc

    start = (state_ref[0:ext, :], jnp.zeros((ext, nf), f32))
    _, leading = lax.fori_loop(0, blocks // BLOCKS, step, start)
    slope, _ = attend(pk_ref, meta_ref, u_ref, 0)
    gs = split(gext_ref[:, 0:size])
    _, du = query_grad(pk_ref, meta_ref, u_ref, slope, gs, split(states_ref[0]), 0)
    pay_ref[0:ext, :] = leading
    pay_ref[ext : ext + FD, :] = jnp.zeros((FD, nf), f32)
    pay_ref[ext : ext + FD, 0:width] = du[:, 0:width]


def inner_kernel(pk_ref, meta_ref, u_ref, gext_ref, states_ref, part_ref, du_ref):
    channels = gext_ref.shape[0] - FD
    size = BLOCKS * pk_ref.shape[2]

    def step(i, nothing):
        span = lanes(i, size)
        slope, p = attend(pk_ref, meta_ref, u_ref, i)
        gs = split(gext_ref[:, span])
        dx, du = query_grad(pk_ref, meta_ref, u_ref, slope, gs, split(states_ref[i]), i)
        du_ref[:, span] = du
        store(part_ref, i, 0, dot3((gs[0][:channels], gs[1][:channels]), p, NT))
        store(part_ref, i, channels, dot3(split(u_ref[:, span]), dx, NT))
        return nothing

    lax.fori_loop(0, pk_ref.shape[0] // BLOCKS, step, 0)


def backward_kernel(pk_ref, meta_ref, taps_ref, part_ref, du_ref, inc_ref, pay_ref, out_ref):
    blocks, width = pk_ref.shape[0], pk_ref.shape[2]
    ext, nf = inc_ref.shape[1:]
    channels = ext - FD
    size = BLOCKS * width
    chunks = blocks // BLOCKS

    def step(count, adjoint):
        i = chunks - 1 - count
        span = lanes(i, size)
        w = key_rows(pk_ref, i).astype(f32)
        vext = value_rows(pk_ref, i)
        tail = meta_ref[2:3, span]
        keep = meta_ref[3:4, span][:, 0:1]
        adj = split(adjoint)
        feat_k = split(phi(w) * tail)
        dfeat = (dot(adj[0], vext, TN) + dot(adj[1], vext, TN)) * tail
        dw = load(part_ref, i, channels, FD) + phi_pullback(w, dfeat)
        store(out_ref, i, channels + FD, 0.5 * dw)
        dv = dot3((adj[0][:channels], adj[1][:channels]), feat_k, NN)
        store(out_ref, i, 0, load(part_ref, i, 0, channels) + dv)
        return keep * adjoint + inc_ref[i]

    lax.fori_loop(0, chunks, step, pay_ref[0:ext, :])
    du = jnp.concatenate([du_ref[...], pay_ref[ext : ext + FD, 0:width]], axis=1) * 0.5
    seq, total = blocks * width, (blocks + 1) * width
    dq = (
        taps_ref[:, 0:1] * du[:, :seq]
        + taps_ref[:, 1:2] * pltpu.roll(du, total - 1, 1)[:, :seq] * meta_ref[6:7, :]
        + taps_ref[:, 2:3] * pltpu.roll(du, total - 2, 1)[:, :seq] * meta_ref[7:8, :]
    )
    for j in range(blocks):
        out_ref[j, channels : channels + FD, :] = dq[:, j * width : (j + 1) * width]


def call(kernel, args, outs, flops):
    shapes = [jax.ShapeDtypeStruct(shape, f32) for shape in outs]
    return pl.pallas_call(
        kernel,
        out_shape=shapes,
        in_specs=[pl.BlockSpec(memory_space=pltpu.VMEM)] * len(args),
        out_specs=[pl.BlockSpec(memory_space=pltpu.VMEM)] * len(outs),
        compiler_params=pltpu.CompilerParams(vmem_limit_bytes=40 * 2**20),
        cost_estimate=pl.CostEstimate(flops=flops, bytes_accessed=2**21, transcendentals=0),
    )(*args)


def meta_rows(seg_ext, width):
    size = BLOCKS * width
    earlier, seg, later = seg_ext[:width], seg_ext[width:-width], seg_ext[-width:]
    last = jnp.repeat(seg[size - 1 :: size], size)
    open_here = earlier[width - 1]
    before = jnp.concatenate([jnp.full((size,), open_here), last[:-size]])
    same = lambda a, b: (a == b).astype(f32)
    late = lambda d: same(jnp.concatenate([earlier[width - d :], seg[:-d]]), seg)
    soon = lambda d: same(jnp.concatenate([seg[d:], later[:d]]), seg)
    rows = [seg, same(seg, before), same(seg, last), same(before, last)]
    rows += [late(1), late(2), soon(1), soon(2)]
    rows += [same(seg, seg[-1]), same(before, open_here)]
    return jnp.pad(jnp.stack(rows), ((0, 6), (0, 0)))


def pack(queries, keys, values):
    heads, length = queries.shape[0] // FD, queries.shape[1]
    shaped = lambda x: x.reshape(heads, -1, length)
    return jnp.concatenate([shaped(queries), shaped(keys), shaped(values.T)], axis=1)


def by_heads(queries, keys, values, seg_ids, conv_weight, out_weight, out_grad):
    heads, length = queries.shape[0] // FD, queries.shape[1]
    groups = [[half * heads + h for h in range(heads)] for half in (0, 1)]
    swap = lambda x: lax.all_to_all(x, "ctx", 0, 0, axis_index_groups=groups)
    onward = lambda x: lax.ppermute(x, "ctx", [(h, h + heads) for h in range(heads)])
    back = lambda x: lax.ppermute(x, "ctx", [(h + heads, h) for h in range(heads)])
    here = lax.axis_index("ctx")
    seq = heads * length
    pk = swap(pack(queries, keys, values))
    everyone = jnp.pad(lax.all_gather(seg_ids, "ctx", tiled=True) + 1, (length, length))
    seg_ext = lax.dynamic_slice_in_dim(everyone, here // heads * seq, seq + 2 * length)
    meta = meta_rows(seg_ext.astype(f32), length)
    grad_attn = lax.dot_general(out_weight, out_grad, NT, preferred_element_type=f32)
    g = swap(grad_attn.reshape(heads, -1, length))
    channels = g.shape[1]
    taps = lax.dynamic_slice_in_dim(conv_weight.astype(f32).T, lax.rem(here, heads) * FD, FD, 0)
    taps = jnp.pad(taps, ((0, 0), (0, 128 - taps.shape[1])))
    ext, nf, chunks = channels + FD, (FD // 2 + 2) * FD, heads // BLOCKS
    work = ext * nf * seq
    (ending,) = call(ending_kernel, (pk, meta), [(ext + FD, nf)], 4 * work)
    u, gext, states, inc, pay = call(
        forward_kernel,
        (pk, g, meta, taps, onward(ending)),
        [(FD, seq), (ext, seq), (chunks, ext, nf), (chunks, ext, nf), (ext + FD, nf)],
        20 * work,
    )
    pay = back(pay)
    part, du = call(
        inner_kernel, (pk, meta, u, gext, states), [(heads, ext, length), (FD, seq)], 20 * work
    )
    (out,) = call(
        backward_kernel,
        (pk, meta, taps, part, du, inc, pay),
        [(heads, ext + FD, length)],
        10 * work,
    )
    out = swap(out)
    return (
        out[:, channels : channels + FD].reshape(heads * FD, length),
        out[:, channels + FD :].reshape(heads * FD, length),
        out[:, :channels].reshape(-1, length).T,
    )


def solution(mesh):
    in_specs = (
        P("head", "ctx"),
        P("head", "ctx"),
        P("ctx", "head"),
        P("ctx"),
        P(None, "head"),
        P("head", None),
        P("ctx", "head"),
    )
    out_specs = (P("head", "ctx"), P("head", "ctx"), P("ctx", "head"))

    def program(queries, *rest):
        heads = queries.shape[0] // FD
        spread = mesh.shape["head"] == 1 and mesh.shape["ctx"] == 2 * heads
        inner = by_heads if spread else body
        return jax.shard_map(
            inner, mesh=mesh, in_specs=in_specs, out_specs=out_specs, check_vma=False
        )(queries, *rest)

    return program
```

```python
import jax
import jax.numpy as jnp
from jax import lax
from jax.experimental import pallas as pl
from jax.experimental.pallas import tpu as pltpu
from jax.sharding import PartitionSpec as P

FD = 16


half_root = 0.7071067811865476
split_mode = lax.Precision.HIGH


def entering(shard, axis, combine, identity, reverse):
    size, here = (lax.axis_size(axis), lax.axis_index(axis))
    everything = jax.tree.map(lambda part: lax.all_gather(part, axis), shard)
    start = jax.tree.map(
        lambda part, zero: jnp.broadcast_to(jnp.asarray(zero, part.dtype), part.shape),
        shard,
        identity,
    )

    def step(k, before):
        at = size - 1 - k if reverse else k
        reached = at > here if reverse else at < here
        new = combine(before, jax.tree.map(lambda part: part[at], everything))
        return jax.tree.map(lambda a, b: jnp.where(reached, a, b), new, before)

    return lax.fori_loop(0, size, step, start)


def features(entries):
    scaled = entries * 0.5
    cross = [
        scaled[..., i : i + 1, :] * scaled[..., i + 1 :, :] for i in range(scaled.shape[-2] - 1)
    ]
    return jnp.concatenate(
        [jnp.ones_like(scaled[..., :1, :]), scaled, scaled * scaled * half_root] + cross, axis=-2
    )


def block_output(q_feat, k_feat, head_values, doc_ids, carry_mask, state_in, normer_in):
    length = doc_ids.shape[0]
    causal = jnp.arange(length)[:, None] >= jnp.arange(length)[None, :]
    allowed = (causal & (doc_ids[:, None] == doc_ids[None, :])).astype(jnp.float32)
    scores = jnp.einsum("hft,hfs->hts", q_feat, k_feat, precision=split_mode) * allowed[None, :, :]
    numerator = jnp.einsum("hts,shd->thd", scores, head_values, precision=split_mode)
    numerator = numerator + carry_mask[:, None, None] * jnp.einsum(
        "hft,hfd->thd", q_feat, state_in, precision=split_mode
    )
    denominator = jnp.sum(scores, axis=2).T + carry_mask[:, None] * jnp.einsum(
        "hft,hf->th", q_feat, normer_in, precision=split_mode
    )
    return numerator / denominator[:, :, None]


def join_forward(earlier, later):
    empty_later = later[0][1] == 0.0
    same_doc = earlier[0][1] == later[0][1]
    state_out = jnp.where(empty_later, earlier[2], later[2] + jnp.where(same_doc, earlier[2], 0.0))
    normer_out = jnp.where(empty_later, earlier[3], later[3] + jnp.where(same_doc, earlier[3], 0.0))
    return (
        jnp.where(empty_later, earlier[0], later[0]),
        jnp.where(empty_later, earlier[1], later[1]),
        state_out,
        normer_out,
    )


def join_backward(earlier, later):
    empty_later = later[0][0] == 0.0
    same_doc = earlier[0][0] == later[0][0]
    state_out = jnp.where(empty_later, earlier[2], later[2] + jnp.where(same_doc, earlier[2], 0.0))
    normer_out = jnp.where(empty_later, earlier[3], later[3] + jnp.where(same_doc, earlier[3], 0.0))
    return (
        jnp.where(empty_later, earlier[0], later[0]),
        jnp.where(empty_later, earlier[1], later[1]),
        state_out,
        normer_out,
    )


def body(queries, keys, values, seg_ids, conv_weight, out_weight, out_grad):
    local_heads = queries.shape[0] // FD
    length = queries.shape[1]
    head_width = values.shape[1] // local_heads
    grad_attn = lax.dot_general(
        lax.all_gather(out_grad, "head", axis=1, tiled=True),
        out_weight,
        (((1,), (1,)), ((), ())),
        preferred_element_type=jnp.float32,
    )
    doc_ids = (seg_ids + 1).astype(jnp.float32)
    query_rows = queries.astype(jnp.float32)
    key_heads = keys.astype(jnp.float32).reshape(local_heads, FD, length)
    head_values = values.astype(jnp.float32).reshape(length, local_heads, head_width)
    taps = conv_weight.astype(jnp.float32)
    k_feat, feature_pullback = jax.vjp(features, key_heads)
    tail_mask = (doc_ids == doc_ids[length - 1]).astype(jnp.float32)
    tail_feat = k_feat * tail_mask[None, None, :]
    tail_state = jnp.einsum("hfs,shd->hfd", tail_feat, head_values, precision=split_mode)
    tail_normer = jnp.sum(tail_feat, axis=2)
    forward_piece = (doc_ids[length - 2 :], query_rows[:, length - 2 :], tail_state, tail_normer)
    before = entering(
        forward_piece, "ctx", join_forward, jax.tree.map(jnp.zeros_like, forward_piece), False
    )
    query_ext = jnp.concatenate([before[1], query_rows], axis=1)
    ids_before = jnp.concatenate([before[0], doc_ids])
    q_conv = taps[0][:, None] * query_rows
    for offset in (1, 2):
        same_doc = (ids_before[2 - offset : 2 - offset + length] == doc_ids).astype(jnp.float32)
        q_conv = (
            q_conv
            + taps[offset][:, None]
            * query_ext[:, 2 - offset : 2 - offset + length]
            * same_doc[None, :]
        )
    carry_mask = (doc_ids == before[0][1]).astype(jnp.float32)

    def local_forward(q_conv_in, k_feat_in, values_in, state_in, normer_in):
        q_feat = features(q_conv_in.reshape(local_heads, FD, length))
        result = block_output(
            q_feat, k_feat_in, values_in, doc_ids, carry_mask, state_in, normer_in
        )
        return result.reshape(length, local_heads * head_width)

    _, local_pullback = jax.vjp(local_forward, q_conv, k_feat, head_values, before[2], before[3])
    grad_qconv, grad_kfeat, grad_heads, grad_state, grad_normer = local_pullback(grad_attn)
    backward_piece = (doc_ids[:2], grad_qconv[:, :2], grad_state, grad_normer)
    after = entering(
        backward_piece, "ctx", join_backward, jax.tree.map(jnp.zeros_like, backward_piece), True
    )
    head_mask = (doc_ids == after[0][0]).astype(jnp.float32)
    flowing = (
        jnp.einsum("hfd,shd->hfs", after[2], head_values, precision=split_mode)
        + after[3][:, :, None]
    )
    grad_kfeat = grad_kfeat + flowing * head_mask[None, None, :]
    grad_heads = grad_heads + jnp.einsum(
        "hfs,hfd->shd", k_feat * head_mask[None, None, :], after[2], precision=split_mode
    )
    (grad_key_heads,) = feature_pullback(grad_kfeat)
    grad_ext = jnp.concatenate([grad_qconv, after[1]], axis=1)
    ids_after = jnp.concatenate([doc_ids, after[0]])
    grad_queries = taps[0][:, None] * grad_qconv
    for offset in (1, 2):
        same_doc = (ids_after[offset : offset + length] == doc_ids).astype(jnp.float32)
        grad_queries = (
            grad_queries
            + taps[offset][:, None] * grad_ext[:, offset : offset + length] * same_doc[None, :]
        )
    grad_keys = grad_key_heads.reshape(local_heads * FD, length)
    grad_values = grad_heads.reshape(length, local_heads * head_width)
    return (grad_queries, grad_keys, grad_values)


f32, bf16 = jnp.float32, jnp.bfloat16
NN = (((1,), (0,)), ((), ()))
NT = (((1,), (1,)), ((), ()))
TN = (((0,), (0,)), ((), ()))
BLOCKS = 2
SEG_ROW = 2 * FD
V_ROW = 3 * FD


def split(x):
    high = x.astype(bf16)
    return high, (x - high.astype(f32)).astype(bf16)


def dot(a, b, dims):
    return lax.dot_general(a, b, dims, preferred_element_type=f32)


def dot3(a, b, dims):
    return dot(a[0], b[0], dims) + dot(a[0], b[1], dims) + dot(a[1], b[0], dims)


def ahead(x, d):
    return pltpu.roll(x, FD - d, 0)


def phi(u):
    rows = [u, u * u * half_root]
    for d in range(1, FD // 2):
        rows.append(u * ahead(u, d))
    half = FD // 2
    one = (lax.broadcasted_iota(jnp.int32, (half, u.shape[1]), 0) == 0).astype(f32)
    rows.append(jnp.concatenate([u[:half] * u[half:], one], axis=0))
    return jnp.concatenate(rows, axis=0)


def phi_pullback(u, grad):
    total = grad[:FD] + (2.0 * half_root) * u * grad[FD : 2 * FD]
    for d in range(1, FD // 2):
        part = grad[(d + 1) * FD : (d + 2) * FD]
        total = total + part * ahead(u, d) + pltpu.roll(part * u, d, 0)
    half = FD // 2
    last = grad[(half + 1) * FD : (half + 1) * FD + half]
    return total + jnp.concatenate([last * u[half:], last * u[:half]], axis=0)


def load(ref, i, start, rows):
    parts = [ref[i * BLOCKS + j, start : start + rows, :] for j in range(BLOCKS)]
    return jnp.concatenate(parts, axis=1)


def store(ref, i, start, x):
    width = ref.shape[2]
    for j in range(BLOCKS):
        ref[i * BLOCKS + j, start : start + x.shape[0], :] = x[:, j * width : (j + 1) * width]


def key_rows(pk_ref, i):
    return load(pk_ref, i, FD, FD) * jnp.asarray(0.5, bf16)


def value_rows(pk_ref, i):
    channels = pk_ref.shape[1] - V_ROW
    values = load(pk_ref, i, V_ROW, channels)
    ones = lax.broadcasted_iota(jnp.int32, (FD, values.shape[1]), 0) == 0
    return jnp.concatenate([values, ones.astype(bf16)], axis=0)


def lanes(i, size):
    return pl.ds(pl.multiple_of(i * size, size), size)


def ending_kernel(pk_ref, meta_ref, state_ref):
    size = BLOCKS * pk_ref.shape[2]

    def step(i, state):
        tail = meta_ref[0:1, lanes(i, size)]
        feat_k = split(phi(key_rows(pk_ref, i).astype(f32)) * tail)
        vext = value_rows(pk_ref, i)
        return state + dot(vext, feat_k[0], NT) + dot(vext, feat_k[1], NT)

    blocks, width = pk_ref.shape[0], pk_ref.shape[2]
    ext, nf = state_ref.shape[0] - FD, state_ref.shape[1]
    state_ref[0:ext, :] = lax.fori_loop(0, blocks // BLOCKS, step, jnp.zeros((ext, nf), f32))
    state_ref[ext : ext + FD, :] = jnp.zeros((FD, nf), f32)
    state_ref[ext : ext + FD, 0:width] = pk_ref[blocks - 1, 0:FD, :].astype(f32)


def attend(pk_ref, meta_ref, u_ref, i):
    size = BLOCKS * pk_ref.shape[2]
    span = lanes(i, size)
    seg_t = jnp.broadcast_to(meta_ref[0:1, span], (size, size))
    causal = lax.broadcasted_iota(jnp.int32, (size, size), 0) <= lax.broadcasted_iota(
        jnp.int32, (size, size), 1
    )
    allowed = jnp.where(causal & (seg_t == seg_t.T), 1.0, 0.0)
    us = split(u_ref[:, span])
    w16 = key_rows(pk_ref, i)
    x = dot(jnp.concatenate([w16, w16], axis=0), jnp.concatenate(us, axis=0), TN)
    return allowed * (1.0 + x), split(allowed * (1.0 + x + 0.5 * x * x))


def query_grad(pk_ref, meta_ref, u_ref, slope, gs, states, i):
    span = lanes(i, BLOCKS * pk_ref.shape[2])
    vext = value_rows(pk_ref, i)
    w16 = key_rows(pk_ref, i)
    dx = split(slope * (dot(vext, gs[0], TN) + dot(vext, gs[1], TN)))
    dfeat = dot3(states, gs, TN) * meta_ref[1:2, span]
    return dx, dot(w16, dx[0], NN) + dot(w16, dx[1], NN) + phi_pullback(u_ref[:, span], dfeat)


def forward_kernel(
    pk_ref, g_ref, meta_ref, taps_ref, state_ref, u_ref, gext_ref, states_ref, inc_ref, pay_ref
):
    blocks, width = pk_ref.shape[0], pk_ref.shape[2]
    channels = g_ref.shape[1]
    ext, nf = channels + FD, state_ref.shape[1]
    size = BLOCKS * width

    raw = [pk_ref[j, 0:FD, :].astype(f32) for j in range(blocks)]
    raw = jnp.concatenate([state_ref[ext : ext + FD, 0:width]] + raw, axis=1) * 0.5
    u_ref[...] = (
        taps_ref[:, 0:1] * raw[:, width:]
        + taps_ref[:, 1:2] * pltpu.roll(raw, 1, 1)[:, width:] * meta_ref[4:5, :]
        + taps_ref[:, 2:3] * pltpu.roll(raw, 2, 1)[:, width:] * meta_ref[5:6, :]
    )

    def step(i, carried):
        state, leading = carried
        span = lanes(i, size)
        vext = value_rows(pk_ref, i)
        keep = meta_ref[3:4, span][:, 0:1]
        first = meta_ref[9:10, span][:, 0:1]
        _, p = attend(pk_ref, meta_ref, u_ref, i)
        feat_q = split(phi(u_ref[:, span]) * meta_ref[1:2, span])
        states_ref[i] = state
        numer = dot(vext, p[0], NN) + dot(vext, p[1], NN) + dot3(split(state), feat_q, NN)
        inverse = 1.0 / numer[channels : channels + 1]
        gp = load(g_ref, i, 0, channels) * inverse
        dden = -jnp.sum(gp * numer[:channels], axis=0, keepdims=True) * inverse
        gext = jnp.concatenate([gp, dden, jnp.zeros((FD - 1, size), f32)], axis=0)
        gext_ref[:, span] = gext
        inc = dot3(split(gext), feat_q, NT)
        inc_ref[i] = inc
        feat_k = split(phi(key_rows(pk_ref, i).astype(f32)) * meta_ref[2:3, span])
        state = keep * state + dot(vext, feat_k[0], NT) + dot(vext, feat_k[1], NT)
        return state, leading + first * inc

    start = (state_ref[0:ext, :], jnp.zeros((ext, nf), f32))
    _, leading = lax.fori_loop(0, blocks // BLOCKS, step, start)
    slope, _ = attend(pk_ref, meta_ref, u_ref, 0)
    gs = split(gext_ref[:, 0:size])
    _, du = query_grad(pk_ref, meta_ref, u_ref, slope, gs, split(states_ref[0]), 0)
    pay_ref[0:ext, :] = leading
    pay_ref[ext : ext + FD, :] = jnp.zeros((FD, nf), f32)
    pay_ref[ext : ext + FD, 0:width] = du[:, 0:width]


def inner_kernel(pk_ref, meta_ref, u_ref, gext_ref, states_ref, part_ref, du_ref):
    channels = gext_ref.shape[0] - FD
    size = BLOCKS * pk_ref.shape[2]

    def step(i, nothing):
        span = lanes(i, size)
        slope, p = attend(pk_ref, meta_ref, u_ref, i)
        gs = split(gext_ref[:, span])
        dx, du = query_grad(pk_ref, meta_ref, u_ref, slope, gs, split(states_ref[i]), i)
        du_ref[:, span] = du
        store(part_ref, i, 0, dot3((gs[0][:channels], gs[1][:channels]), p, NT))
        store(part_ref, i, channels, dot3(split(u_ref[:, span]), dx, NT))
        return nothing

    lax.fori_loop(0, pk_ref.shape[0] // BLOCKS, step, 0)


def backward_kernel(pk_ref, meta_ref, taps_ref, part_ref, du_ref, inc_ref, pay_ref, out_ref):
    blocks, width = pk_ref.shape[0], pk_ref.shape[2]
    ext, nf = inc_ref.shape[1:]
    channels = ext - FD
    size = BLOCKS * width
    chunks = blocks // BLOCKS

    def step(count, adjoint):
        i = chunks - 1 - count
        span = lanes(i, size)
        w = key_rows(pk_ref, i).astype(f32)
        vext = value_rows(pk_ref, i)
        tail = meta_ref[2:3, span]
        keep = meta_ref[3:4, span][:, 0:1]
        adj = split(adjoint)
        feat_k = split(phi(w) * tail)
        dfeat = (dot(adj[0], vext, TN) + dot(adj[1], vext, TN)) * tail
        dw = load(part_ref, i, channels, FD) + phi_pullback(w, dfeat)
        store(out_ref, i, channels + FD, 0.5 * dw)
        dv = dot3((adj[0][:channels], adj[1][:channels]), feat_k, NN)
        store(out_ref, i, 0, load(part_ref, i, 0, channels) + dv)
        return keep * adjoint + inc_ref[i]

    lax.fori_loop(0, chunks, step, pay_ref[0:ext, :])
    du = jnp.concatenate([du_ref[...], pay_ref[ext : ext + FD, 0:width]], axis=1) * 0.5
    seq, total = blocks * width, (blocks + 1) * width
    dq = (
        taps_ref[:, 0:1] * du[:, :seq]
        + taps_ref[:, 1:2] * pltpu.roll(du, total - 1, 1)[:, :seq] * meta_ref[6:7, :]
        + taps_ref[:, 2:3] * pltpu.roll(du, total - 2, 1)[:, :seq] * meta_ref[7:8, :]
    )
    for j in range(blocks):
        out_ref[j, channels : channels + FD, :] = dq[:, j * width : (j + 1) * width]


def call(kernel, args, outs, flops):
    shapes = [jax.ShapeDtypeStruct(shape, f32) for shape in outs]
    return pl.pallas_call(
        kernel,
        out_shape=shapes,
        in_specs=[pl.BlockSpec(memory_space=pltpu.VMEM)] * len(args),
        out_specs=[pl.BlockSpec(memory_space=pltpu.VMEM)] * len(outs),
        compiler_params=pltpu.CompilerParams(vmem_limit_bytes=40 * 2**20),
        cost_estimate=pl.CostEstimate(flops=flops, bytes_accessed=2**21, transcendentals=0),
    )(*args)


def meta_rows(seg_ext, width):
    size = BLOCKS * width
    earlier, seg, later = seg_ext[:width], seg_ext[width:-width], seg_ext[-width:]
    last = jnp.repeat(seg[size - 1 :: size], size)
    open_here = earlier[width - 1]
    before = jnp.concatenate([jnp.full((size,), open_here), last[:-size]])
    same = lambda a, b: (a == b).astype(f32)
    late = lambda d: same(jnp.concatenate([earlier[width - d :], seg[:-d]]), seg)
    soon = lambda d: same(jnp.concatenate([seg[d:], later[:d]]), seg)
    rows = [seg, same(seg, before), same(seg, last), same(before, last)]
    rows += [late(1), late(2), soon(1), soon(2)]
    rows += [same(seg, seg[-1]), same(before, open_here)]
    return jnp.pad(jnp.stack(rows), ((0, 6), (0, 0)))


def pack(queries, keys, values, seg_ids):
    heads, length = queries.shape[0] // FD, queries.shape[1]
    shaped = lambda x: x.reshape(heads, -1, length)
    seg = jnp.broadcast_to((seg_ids + 1).astype(bf16), (heads, FD, length))
    return jnp.concatenate([shaped(queries), shaped(keys), seg, shaped(values.T)], axis=1)


def by_heads(queries, keys, values, seg_ids, conv_weight, out_weight, out_grad):
    heads, length = queries.shape[0] // FD, queries.shape[1]
    groups = [[half * heads + h for h in range(heads)] for half in (0, 1)]
    swap = lambda x: lax.all_to_all(x, "ctx", 0, 0, axis_index_groups=groups)
    onward = lambda x: lax.ppermute(x, "ctx", [(h, h + heads) for h in range(heads)])
    back = lambda x: lax.ppermute(x, "ctx", [(h + heads, h) for h in range(heads)])
    here = lax.axis_index("ctx")
    seq = heads * length
    pk = swap(pack(queries, keys, values, seg_ids))
    edge_before = onward(pk[-1, SEG_ROW:V_ROW])[0]
    edge_after = back(pk[0, SEG_ROW:V_ROW])[0]
    seg = pk[:, SEG_ROW].reshape(-1)
    open_end = jnp.broadcast_to((seg == seg[-1]).astype(f32), (FD, seq))
    seg_ext = jnp.concatenate([edge_before, seg, edge_after])
    meta = meta_rows(seg_ext.astype(f32), length)
    grad_attn = lax.dot_general(out_weight, out_grad, NT, preferred_element_type=f32)
    g = swap(grad_attn.reshape(heads, -1, length))
    channels = g.shape[1]
    taps = lax.dynamic_slice_in_dim(conv_weight.astype(f32).T, lax.rem(here, heads) * FD, FD, 0)
    taps = jnp.pad(taps, ((0, 0), (0, 128 - taps.shape[1])))
    ext, nf, chunks = channels + FD, (FD // 2 + 2) * FD, heads // BLOCKS
    work = ext * nf * seq
    (ending,) = call(ending_kernel, (pk, open_end), [(ext + FD, nf)], 4 * work)
    u, gext, states, inc, pay = call(
        forward_kernel,
        (pk, g, meta, taps, onward(ending)),
        [(FD, seq), (ext, seq), (chunks, ext, nf), (chunks, ext, nf), (ext + FD, nf)],
        20 * work,
    )
    pay = back(pay)
    part, du = call(
        inner_kernel, (pk, meta, u, gext, states), [(heads, ext, length), (FD, seq)], 20 * work
    )
    (out,) = call(
        backward_kernel,
        (pk, meta, taps, part, du, inc, pay),
        [(heads, ext + FD, length)],
        10 * work,
    )
    out = swap(out)
    return (
        out[:, channels : channels + FD].reshape(heads * FD, length),
        out[:, channels + FD :].reshape(heads * FD, length),
        out[:, :channels].reshape(-1, length).T,
    )


def solution(mesh):
    in_specs = (
        P("head", "ctx"),
        P("head", "ctx"),
        P("ctx", "head"),
        P("ctx"),
        P(None, "head"),
        P("head", None),
        P("ctx", "head"),
    )
    out_specs = (P("head", "ctx"), P("head", "ctx"), P("ctx", "head"))

    def program(queries, *rest):
        heads = queries.shape[0] // FD
        spread = mesh.shape["head"] == 1 and mesh.shape["ctx"] == 2 * heads
        inner = by_heads if spread else body
        return jax.shard_map(
            inner, mesh=mesh, in_specs=in_specs, out_specs=out_specs, check_vma=False
        )(queries, *rest)

    return program
```
